128 devices in a mesh: row: 8 (over z_hi, y), col: 16 (over z_lo, x, core).
Axes of the slice: x: 4, y: 4, z: 4 (z_hi: 2, z_lo: 2; z = z_hi * 2 + z_lo), core: 2. Of those that a mesh axis runs over, the one named last changes fastest.
Arguments:
- pair: bfloat16 [1024, 1024, 128], P('row', 'col'), may hold values from -6 to 6
- ln_gain: float32 [128], replicated, may hold values from 0.1 to 1.9
- w_query: bfloat16 [128, 128], replicated, may hold values from -21.213203 to 21.213203
- w_key: bfloat16 [128, 128], replicated, may hold values from -0.5 to 0.5
- w_value: bfloat16 [128, 128], replicated, may hold values from -0.5 to 0.5
- w_gate: bfloat16 [128, 128], replicated, may hold values from -0.5 to 0.5
- w_bias: bfloat16 [128, 4], replicated, may hold values from -1.0546875 to 1.0546875
- w_out: bfloat16 [128, 128], replicated, may hold values from -1.5 to 1.5
Outputs:
- update: bfloat16 [1024, 1024, 128], P('row', 'col')
The draws below stay inside these ranges and needn't reach their ends.
All inputs are finite; a program needn't handle non-finite values.
Results may differ from the reference program's by a relative error of at most 0.009.
The reference program's roundings to bfloat16 on the way (of `normed`, `query`, `keys`, `values`, `tri_bias`, `rounded` and `gated`) count: a program that leaves them out, or rounds other values in their place, can miss the bound.
Values may be sent and summed in bfloat16 or wider, within the bound.
A program may use at most 256 MiB of HBM per device.

```python
import math
import jax
import jax.numpy as jnp
from jax import lax

D = 128
HEADS = 4
HEAD_DIM = 32
RESIDUES = 1024


def draw_w_query(key, part):
    key = jax.random.fold_in(key, 11)
    base = jax.random.truncated_normal(key, -6.0, 6.0, (D, HEADS * HEAD_DIM), jnp.float32) * D ** (-0.5)
    return base.astype(jnp.bfloat16)


def level_of(rng, dims, cuts, least, largest):
    loudness = 1.0
    for position, parts in cuts:
        draws = jax.random.uniform(jax.random.fold_in(jax.random.fold_in(rng, 6), position), (parts,), jnp.float32, least / len(cuts), largest / len(cuts))
        loudness = loudness * jnp.repeat(jnp.exp(draws), dims[position] // parts).reshape((-1,) + (1,) * (len(dims) - 1 - position))
    return loudness


def noise(key, extent, scale, limit, shards=(), kind=jnp.bfloat16):
    result = scale * jax.random.normal(key, extent, jnp.float32)
    if shards:
        result = result * level_of(key, extent, shards, -0.22, 0.18)
    return jnp.clip(result, -limit, limit).astype(kind)


def setup_inputs(seed: int = 0) -> dict:
    key_list = jax.random.split(jax.random.key(seed), 9)
    return {
        "pair": noise(key_list[0], (RESIDUES, RESIDUES, D), 1.0, 6.0, ((0, 8), (1, 16))),
        "ln_gain": jnp.clip(1.0 + 0.18 * jax.random.normal(key_list[1], (D,), jnp.float32), 0.1, 1.9),
        "w_query": draw_w_query(jax.random.fold_in(key_list[8], 71), 0),
        "w_key": noise(key_list[3], (D, HEADS * HEAD_DIM), D ** -0.5, 0.5),
        "w_value": noise(key_list[4], (D, HEADS * HEAD_DIM), D ** -0.5, 0.5),
        "w_gate": noise(key_list[5], (D, HEADS * HEAD_DIM), D ** -0.5, 0.5),
        "w_bias": noise(key_list[6], (D, HEADS), (2.0 * D ** -0.5), 1.0546875),
        "w_out": noise(key_list[7], (HEADS * HEAD_DIM, D), (HEADS * HEAD_DIM // 8) ** -0.5, 1.5),
    }


def layer_norm(tile, gain):
    values = tile.astype(jnp.float32)
    center = lax.optimization_barrier(jnp.mean(values, axis=-1, keepdims=True))
    spread = lax.optimization_barrier(jnp.mean(jnp.square(values - center), axis=-1, keepdims=True))
    return ((values - center) * lax.rsqrt(spread + 1e-05) * gain.astype(jnp.float32)).astype(jnp.bfloat16)

def reference(pair, ln_gain, w_query, w_key, w_value, w_gate, w_bias, w_out):
    normed = layer_norm(pair, ln_gain)
    scale = 1.0 / math.sqrt(HEAD_DIM)
    shape4 = (RESIDUES, RESIDUES, HEADS, HEAD_DIM)
    query = (jnp.dot(normed, w_query, preferred_element_type=jnp.float32) * scale).astype(jnp.bfloat16).reshape(shape4)
    keys = jnp.dot(normed, w_key, preferred_element_type=jnp.float32).astype(jnp.bfloat16).reshape(shape4)
    values = jnp.dot(normed, w_value, preferred_element_type=jnp.float32).astype(jnp.bfloat16).reshape(shape4)
    gate = jax.nn.sigmoid(jnp.dot(normed, w_gate, preferred_element_type=jnp.float32))
    tri_bias = jnp.transpose(jnp.dot(normed, w_bias, preferred_element_type=jnp.float32).astype(jnp.bfloat16), (0, 2, 1)).astype(jnp.float32)
    block_rows = 8

    def one_block(index):
        begin = (index * block_rows).astype(jnp.int32)
        q_rows = lax.dynamic_slice_in_dim(query, begin, block_rows, 0).astype(jnp.float32)
        k_rows = lax.dynamic_slice_in_dim(keys, begin, block_rows, 0).astype(jnp.float32)
        v_rows = lax.dynamic_slice_in_dim(values, begin, block_rows, 0).astype(jnp.float32)
        g_rows = lax.dynamic_slice_in_dim(gate, begin, block_rows, 0)
        scores = jnp.einsum('abhe,akhe->abhk', q_rows, k_rows) + tri_bias[None]
        most = lax.optimization_barrier(jnp.max(scores, axis=-1, keepdims=True))
        weights = jnp.exp(scores - most)
        denom = lax.optimization_barrier(jnp.sum(weights, axis=-1))
        rounded = lax.optimization_barrier(weights.astype(jnp.bfloat16)).astype(jnp.float32)
        attended = jnp.einsum('abhk,akhe->abhe', rounded, v_rows) / denom[..., None]
        attended = attended.reshape(block_rows, RESIDUES, HEADS * HEAD_DIM)
        gated = (g_rows * attended).astype(jnp.bfloat16)
        return jnp.dot(gated, w_out, preferred_element_type=jnp.float32).astype(jnp.bfloat16)
    blocks = lax.map(one_block, jnp.arange(RESIDUES // block_rows, dtype=jnp.int32))
    return blocks.reshape(RESIDUES, RESIDUES, D)
```

```python
import math

import jax
import jax.numpy as jnp
from jax import lax
from jax.experimental import pallas as pl
from jax.experimental.pallas import tpu as pltpu
from jax.sharding import PartitionSpec as P

F32 = jnp.float32
BF16 = jnp.bfloat16
MESH = pl.DeviceIdType.MESH

HEADS = 4
HEAD_DIM = 32
D = 128
RES = 1024
ROWS, COLS = 8, 16
BAND = RES // ROWS
KEYS = RES // COLS
MINE = BAND // COLS
SLOTS = 8
HALF = RES // 2
PARTS = 4
KC = RES // PARTS
RC = HALF // PARTS


def layer_norm(tile, gain):
    values = tile.astype(F32)
    center = jnp.mean(values, axis=-1, keepdims=True)
    offset = values - center
    spread = jnp.mean(offset * offset, axis=-1, keepdims=True)
    return offset * lax.rsqrt(spread + 1e-05) * gain


def remote(src, dst, send, recv, row, col):
    return pltpu.make_async_remote_copy(
        src_ref=src, dst_ref=dst, send_sem=send, recv_sem=recv,
        device_id={"row": row, "col": col}, device_id_type=MESH,
    )


def kernel(
    x_ref, gain_ref, wq_ref, wk_ref, wv_ref, wg_ref, wb_ref, wo_ref, o_ref,
    got, piece_f, piece, bands, bias, w_all, q_s, k_s, v_s, g_s, s_s, p_s, acc_s, out_s,
    x_send, x_recv, x_own, b_send, b_recv, b_own, r_send, r_recv, c_send, c_recv, o_send, o_recv, o_own,
):
    row, col = lax.axis_index("row"), lax.axis_index("col")
    zh, y, core = row // 4, row % 4, col % 2
    row_z = (1 - zh) * 4 + y
    row_1 = zh * 4 + y + 1 - 2 * (y % 2)
    row_3 = zh * 4 + 3 - y
    col_c = col + 1 - 2 * core

    barrier = pltpu.get_barrier_semaphore()
    for d in range(1, COLS):
        pl.semaphore_signal(barrier, inc=1, device_id={"row": row, "col": (col + d) % COLS}, device_id_type=MESH)
    for other in (row_z, row_1, row_3):
        pl.semaphore_signal(barrier, inc=1, device_id={"row": other, "col": col}, device_id_type=MESH)
    pl.semaphore_wait(barrier, COLS - 1 + 3)

    own_keys = pl.ds(pl.multiple_of(col * KEYS, KEYS), KEYS)
    x_copies = []
    for part in range(2):
        for d in range(1, COLS):
            to = (col + d) % COLS
            copy = remote(
                x_ref.at[pl.ds(to * MINE + part * 4, 4)], got.at[pl.ds(part * 4, 4), own_keys],
                x_send.at[part, d], x_recv.at[part, d], row, to,
            )
            copy.start()
            x_copies.append(copy)
    x_local = pltpu.make_async_copy(x_ref.at[pl.ds(col * MINE, MINE)], got.at[:, own_keys], x_own)
    x_local.start()

    gain = gain_ref[...]

    @pl.loop(0, 8)
    def _(i):
        tile = x_ref[pl.ds(i * 16, 16)].reshape(16 * KEYS, D)
        g_s[pl.ds(pl.multiple_of(i * 16 * KEYS, 16 * KEYS), 16 * KEYS)] = layer_norm(tile, gain)

    @pl.loop(0, KEYS, unroll=8)
    def _(k):
        normed = g_s[pl.ds(k, BAND, stride=KEYS), :].astype(BF16)
        out = lax.dot_general(wb_ref[...], normed, (((1,), (1,)), ((), ())), preferred_element_type=F32)
        for h in range(HEADS):
            piece_f[h, pl.ds(k, 1)] = out[h : h + 1]

    piece[...] = piece_f[...].astype(BF16)

    b_copies = []
    for d in range(1, COLS):
        to = (col + d) % COLS
        heads = pl.ds((to % 2) * 2, 2)
        copy = remote(piece.at[heads], bands.at[0, heads, own_keys], b_send.at[d], b_recv.at[d], row, to)
        copy.start()
        b_copies.append(copy)
    mine = pl.ds(core * 2, 2)
    b_local = pltpu.make_async_copy(piece.at[mine], bands.at[0, mine, own_keys], b_own)
    b_local.start()

    w_all[:, 0:128] = wq_ref[...]
    w_all[:, 128:256] = wk_ref[...]
    w_all[:, 256:384] = wv_ref[...]
    w_all[:, 384:512] = wg_ref[...]
    v_s[:, :, 128:] = jnp.ones((MINE, RES, 128), BF16)
    p_s[1] = jnp.ones((HALF, RES), BF16)

    b_local.wait()
    for copy in b_copies:
        copy.wait_recv()

    def band(slot):
        return bands.at[slot, mine]

    def relay(src, dst, to_row, index):
        return remote(band(src), band(dst), r_send.at[index], r_recv.at[dst], to_row, col)

    def share(slot):
        return remote(band(slot), band(slot), c_send.at[slot], c_recv.at[slot], row, col_c)

    relays = [
        relay(0, 1, row_z, 0), relay(0, 2, row_1, 1), relay(0, 4, row_3, 2),
        relay(1, 3, row_1, 3), relay(1, 5, row_3, 4),
        relay(3, 7, row_3, 5), relay(4, 6, row_1, 6),
    ]
    shares = [share(slot) for slot in range(SLOTS)]
    landed = {1: relays[0], 2: relays[1], 3: relays[3], 4: relays[2], 5: relays[4], 6: relays[6], 7: relays[5]}

    relays[0].start()
    relays[1].start()
    relays[2].start()
    shares[0].start()

    lane = lax.broadcasted_iota(jnp.int32, (1, D), 1)
    own_lanes = [(lane >= HEAD_DIM * h) & (lane < HEAD_DIM * (h + 1)) for h in range(HEADS)]

    def slot_of(band_row):
        z, w = band_row // 4, band_row % 4
        odd, high = (w + y) % 2, (w // 2 + y // 2) % 2
        return (z + zh) % 2 + 2 * (2 * high + (odd + high) % 2)

    def project(first):
        @pl.loop(first, first + 4)
        def _(a):
            normed = layer_norm(got[a], gain).astype(BF16)
            mixed = jnp.dot(normed, w_all[...], preferred_element_type=F32)
            query = (mixed[:, 0:128] * (1.0 / math.sqrt(HEAD_DIM))).astype(BF16)
            k_s[a] = mixed[:, 128:256].astype(BF16)
            v_s[a, :, 0:128] = mixed[:, 256:384].astype(BF16)
            gate = jax.nn.sigmoid(mixed[:, 384:512])
            for r in range(ROWS):
                begin = pl.multiple_of(slot_of(r) * BAND, BAND)
                part = query[r * BAND : (r + 1) * BAND]
                for h in range(HEADS):
                    q_s[a, h, pl.ds(begin, BAND)] = jnp.where(own_lanes[h], part, jnp.zeros_like(part))
                g_s[pl.ds(pl.multiple_of(a * RES + begin, BAND), BAND)] = gate[r * BAND : (r + 1) * BAND]

    x_local.wait()
    for copy in x_copies[: COLS - 1]:
        copy.wait_recv()
    project(0)

    landed[1].wait_recv()
    relays[3].start()
    relays[4].start()
    shares[1].start()

    for copy in x_copies[COLS - 1 :]:
        copy.wait_recv()
    project(4)

    landed[2].wait_recv()
    shares[2].start()
    landed[4].wait_recv()
    relays[6].start()
    shares[4].start()
    landed[3].wait_recv()
    relays[5].start()
    shares[3].start()

    def take_bias(phase):
        for slot in range(4):
            shares[phase * 4 + slot].wait_recv()

        @pl.loop(0, HEADS)
        def _(h):
            for slot in range(4):
                for j in range(RES // 128):
                    block = bands[phase * 4 + slot, h, j * 128 : (j + 1) * 128].astype(F32)
                    bias[h, slot * BAND : (slot + 1) * BAND, j * 128 : (j + 1) * 128] = block.T

    def scores(step, h, j):
        phase, a = step // MINE, step % MINE
        rows = pl.ds(pl.multiple_of(phase * HALF, HALF), HALF)
        s_s[h % 2, :, j * KC : (j + 1) * KC] = lax.dot_general(
            q_s[a, h, rows], k_s[a, j * KC : (j + 1) * KC], (((1,), (1,)), ((), ())), preferred_element_type=F32
        )

    def soften(h, j):
        rows = slice(j * RC, (j + 1) * RC)
        logits = s_s[h % 2, rows] + bias[h, rows]
        most = jnp.max(logits, axis=-1, keepdims=True)
        p_s[h % 2, rows] = jnp.exp(logits - most).astype(BF16)

    def attend(step, h, j, total):
        a = step % MINE
        part = jnp.dot(
            p_s[h % 2, :, j * KC : (j + 1) * KC], v_s[a, j * KC : (j + 1) * KC], preferred_element_type=F32
        )
        return part if total is None else total + part

    def settle(total, h):
        head = total[:, 0:128] / total[:, 128:256]
        acc_s[...] = head if h == 0 else jnp.where(own_lanes[h], head, acc_s[...])

    def produce(step):
        phase, a = step // MINE, step % MINE
        begin = pl.multiple_of(phase * HALF, HALF)
        gate = g_s[pl.ds(pl.multiple_of(a * RES + begin, HALF), HALF)]
        gated = (gate * acc_s[...]).astype(BF16)
        out_s[a, pl.ds(begin, HALF)] = jnp.dot(gated, wo_ref[...], preferred_element_type=F32).astype(BF16)

    band_rows = [row, row_z, row_1, (1 - zh) * 4 + row_1 % 4, row_3, (1 - zh) * 4 + row_3 % 4,
                 zh * 4 + (y + 2) % 4, (1 - zh) * 4 + (y + 2) % 4]

    def deliver(step):
        phase, a = step // MINE, step % MINE
        for slot in range(4):
            owner = jnp.where(phase == 0, band_rows[slot], band_rows[slot + 4])
            for half in range(2):
                to = owner * 2 + half
                begin = pl.multiple_of((phase * 4 + slot) * BAND + half * KEYS, KEYS)
                src, dst = out_s.at[a, pl.ds(begin, KEYS)], o_ref.at[col * MINE + a]

                @pl.when(to != col)
                def _():
                    remote(src, dst, o_send.at[to], o_recv.at[col], row, to).start()

                @pl.when(to == col)
                def _():
                    pltpu.make_async_copy(src, dst, o_own).start()

    take_bias(0)
    for j in range(PARTS):
        scores(0, 0, j)

    @pl.loop(0, 2 * MINE)
    def _(step):
        before = (step + 2 * MINE - 1) % (2 * MINE)
        after = (step + 1) % (2 * MINE)

        @pl.when(step == 4)
        def _():
            for slot in (5, 6, 7):
                landed[slot].wait_recv()
                shares[slot].start()

        @pl.when(step == MINE)
        def _():
            take_bias(1)

        for h in range(HEADS):
            total = None
            for j in range(PARTS):
                if h < HEADS - 1:
                    scores(step, h + 1, j)
                else:
                    scores(after, 0, j)
                soften(h, j)
                total = attend(step if h else before, (h - 1) % HEADS, j, total)
            settle(total, (h - 1) % HEADS)
            if h == 0:
                produce(before)

        @pl.when(step > 0)
        def _():
            deliver(before)

    last = 2 * MINE - 1
    total = None
    for j in range(PARTS):
        total = attend(last, HEADS - 1, j, total)
    settle(total, HEADS - 1)
    produce(last)
    deliver(last)

    for copy in x_copies + b_copies + relays + shares:
        copy.wait_send()
    for d in range(1, COLS):
        other = (col + d) % COLS
        block = o_ref.at[pl.ds(other * MINE, MINE)]
        remote(block, block, o_send.at[other], o_recv.at[other], row, other).wait()
    block = o_ref.at[pl.ds(col * MINE, MINE)]
    pltpu.make_async_copy(block, block, o_own).wait()


def shards(pair, ln_gain, w_query, w_key, w_value, w_gate, w_bias, w_out):
    dma = pltpu.SemaphoreType.DMA
    vmem = pl.BlockSpec(memory_space=pltpu.VMEM)
    return pl.pallas_call(
        kernel,
        out_shape=jax.ShapeDtypeStruct(pair.shape, BF16),
        in_specs=[vmem] * 8,
        out_specs=pl.BlockSpec(memory_space=pl.ANY),
        scratch_shapes=[
            pltpu.VMEM((MINE, RES, D), BF16),
            pltpu.VMEM((HEADS, KEYS, BAND), F32),
            pltpu.VMEM((HEADS, KEYS, BAND), BF16),
            pltpu.VMEM((SLOTS, HEADS, RES, BAND), BF16),
            pltpu.VMEM((HEADS, HALF, RES), F32),
            pltpu.VMEM((D, 4 * D), BF16),
            pltpu.VMEM((MINE, HEADS, RES, D), BF16),
            pltpu.VMEM((MINE, RES, D), BF16),
            pltpu.VMEM((MINE, RES, 2 * D), BF16),
            pltpu.VMEM((MINE * RES, D), F32),
            pltpu.VMEM((2, HALF, RES), F32),
            pltpu.VMEM((2, HALF, RES), BF16),
            pltpu.VMEM((HALF, D), F32),
            pltpu.VMEM((MINE, RES, D), BF16),
            dma((2, COLS)), dma((2, COLS)), dma,
            dma((COLS,)), dma((COLS,)), dma,
            dma((7,)), dma((SLOTS,)),
            dma((SLOTS,)), dma((SLOTS,)),
            dma((COLS,)), dma((COLS,)), dma,
        ],
        compiler_params=pltpu.CompilerParams(
            collective_id=0, has_side_effects=True, vmem_limit_bytes=60 << 20
        ),
    )(
        pair, ln_gain.reshape(1, -1), w_query, w_key, w_value, w_gate,
        jnp.pad(w_bias.T, ((0, 8 - HEADS), (0, 0))), w_out,
    )


def solution(mesh):
    return jax.shard_map(
        shards,
        mesh=mesh,
        in_specs=(P("row", "col", None), P(), P(), P(), P(), P(), P(), P()),
        out_specs=P("row", "col", None),
        check_vma=False,
    )
```

```python
import math

import jax
import jax.numpy as jnp
from jax import lax
from jax.experimental import pallas as pl
from jax.experimental.pallas import tpu as pltpu
from jax.sharding import PartitionSpec as P

F32 = jnp.float32
BF16 = jnp.bfloat16
MESH = pl.DeviceIdType.MESH

HEADS = 4
HEAD_DIM = 32
D = 128
RES = 1024
ROWS, COLS = 8, 16
BAND = RES // ROWS
KEYS = RES // COLS
MINE = BAND // COLS
SLOTS = 8
HALF = RES // 2
PARTS = 4
KC = RES // PARTS
RC = HALF // PARTS
ROW_PARTS = [(0, 3), (3, 2), (5, 2), (7, 1)]
ORDER = [
    (1, 2, 0), (0, 1, 0), (1, 0, 0), (0, 3, 0), (1, 1, 0), (0, 2, 0), (1, 3, 0),
    (1, 2, 1), (0, 1, 1), (1, 0, 1), (0, 3, 1), (1, 1, 1), (0, 2, 1), (1, 3, 1), (0, 0, 1),
]


def layer_norm(tile, gain):
    values = tile.astype(F32)
    center = jnp.mean(values, axis=-1, keepdims=True)
    offset = values - center
    spread = jnp.mean(offset * offset, axis=-1, keepdims=True)
    return offset * lax.rsqrt(spread + 1e-05) * gain


def remote(src, dst, send, recv, row, col):
    return pltpu.make_async_remote_copy(
        src_ref=src, dst_ref=dst, send_sem=send, recv_sem=recv,
        device_id={"row": row, "col": col}, device_id_type=MESH,
    )


def kernel(
    x_ref, gain_ref, wq_ref, wk_ref, wv_ref, wg_ref, wb_ref, wo_ref, o_ref,
    got, piece_f, piece, bands, bias, w_all, q_s, k_s, v_s, g_s, s_s, p_s, m_s, acc_s, out_s,
    x_send, x_recv, x_own, b_send, b_recv, b_own, r_send, r_recv, c_send, c_recv, o_send, o_recv, o_own,
):
    row, col = lax.axis_index("row"), lax.axis_index("col")
    zh, y, core = row // 4, row % 4, col % 2
    row_z = (1 - zh) * 4 + y
    row_1 = zh * 4 + y + 1 - 2 * (y % 2)
    row_3 = zh * 4 + 3 - y
    col_c = col + 1 - 2 * core
    col_z = (col + 8) % COLS

    barrier = pltpu.get_barrier_semaphore()
    for d in range(1, COLS):
        pl.semaphore_signal(barrier, inc=1, device_id={"row": row, "col": (col + d) % COLS}, device_id_type=MESH)
    for other, at in ((row_z, col_z), (row_1, col), (row_3, col)):
        pl.semaphore_signal(barrier, inc=1, device_id={"row": other, "col": at}, device_id_type=MESH)
    pl.semaphore_wait(barrier, COLS - 1 + 3)

    own_keys = pl.ds(pl.multiple_of(col * KEYS, KEYS), KEYS)
    z_low, x_at = col // 8, (col // 2) % 4
    others = [
        ((z_low + dz) % 2) * 8 + ((x_at + dx) % 4) * 2 + (core + dc) % 2 for dz, dx, dc in ORDER
    ]

    def exchange(part):
        first, count = ROW_PARTS[part]
        return [
            remote(
                x_ref.at[pl.ds(to * MINE + first, count)], got.at[pl.ds(first, count), own_keys],
                x_send.at[part, index], x_recv.at[part, index], row, to,
            )
            for index, to in enumerate(others)
        ]

    x_copies = [exchange(part) for part in range(4)]
    for copy in x_copies[0]:
        copy.start()
    x_local = pltpu.make_async_copy(x_ref.at[pl.ds(col * MINE, MINE)], got.at[:, own_keys], x_own)
    x_local.start()

    gain = gain_ref[...]
    acc_s[0:D] = jnp.zeros((D, D), F32)
    acc_s[0:D, 0:HEADS] = wb_ref[...].astype(F32)
    w_bias = acc_s[0:D].T[0:8].astype(BF16)

    @pl.loop(0, 8)
    def _(i):
        tile = x_ref[pl.ds(i * 16, 16)].reshape(16 * KEYS, D)
        g_s[pl.ds(pl.multiple_of(i * 16 * KEYS, 16 * KEYS), 16 * KEYS)] = layer_norm(tile, gain)

    @pl.loop(0, KEYS, unroll=8)
    def _(k):
        normed = g_s[pl.ds(k, BAND, stride=KEYS), :].astype(BF16)
        out = lax.dot_general(w_bias, normed, (((1,), (1,)), ((), ())), preferred_element_type=F32)
        for h in range(HEADS):
            piece_f[h, pl.ds(k, 1)] = out[h : h + 1]

    piece[...] = piece_f[...].astype(BF16)

    b_copies = []
    for index, to in enumerate(others):
        heads = pl.ds((to % 2) * 2, 2)
        copy = remote(piece.at[heads], bands.at[0, heads, own_keys], b_send.at[index], b_recv.at[index], row, to)
        copy.start()
        b_copies.append(copy)
    mine = pl.ds(core * 2, 2)
    b_local = pltpu.make_async_copy(piece.at[mine], bands.at[0, mine, own_keys], b_own)
    b_local.start()

    w_all[:, 0:128] = wq_ref[...]
    w_all[:, 128:256] = wk_ref[...]
    w_all[:, 256:384] = wv_ref[...]
    w_all[:, 384:512] = wg_ref[...]
    v_s[:, :, 128:] = jnp.ones((MINE, RES, 128), BF16)
    p_s[1] = jnp.ones((HALF, RES), BF16)

    b_local.wait()
    for copy in b_copies:
        copy.wait_recv()

    def band(slot):
        return bands.at[slot, mine]

    def relay(src, dst, to_row, index, to_col=col):
        return remote(band(src), band(dst), r_send.at[index], r_recv.at[dst], to_row, to_col)

    def share(slot):
        return remote(band(slot), band(slot), c_send.at[slot], c_recv.at[slot], row, col_c)

    relays = {
        1: relay(0, 1, row_z, 0, col_z), 2: relay(0, 2, row_1, 1), 3: relay(0, 3, row_3, 2),
        4: relay(1, 4, row_1, 3), 5: relay(1, 5, row_3, 4), 6: relay(3, 6, row_1, 5), 7: relay(4, 7, row_3, 6),
    }
    shares = [share(slot) for slot in range(SLOTS)]

    def arrive(slot, *onward):
        relays[slot].wait_recv()
        for then in onward:
            relays[then].start()
        shares[slot].start()

    for slot in (1, 2, 3):
        relays[slot].start()
    shares[0].start()
    for part in (1, 2, 3):
        for copy in x_copies[part]:
            copy.start()

    lane = lax.broadcasted_iota(jnp.int32, (1, D), 1)
    own_lanes = [(lane >= HEAD_DIM * h) & (lane < HEAD_DIM * (h + 1)) for h in range(HEADS)]

    def slot_of(band_row):
        z, w = band_row // 4, band_row % 4
        far, odd, high = (z + zh) % 2, (w + y) % 2, (w // 2 + y // 2) % 2
        near = odd * (2 + high + 2 * far)
        return near + (1 - odd) * (far + 6 * high)

    def project(part):
        for copy in x_copies[part]:
            copy.wait_recv()

        first, count = ROW_PARTS[part]

        @pl.loop(first, first + count)
        def _(a):
            normed = layer_norm(got[a], gain).astype(BF16)
            mixed = jnp.dot(normed, w_all[...], preferred_element_type=F32)
            query = (mixed[:, 0:128] * (1.0 / math.sqrt(HEAD_DIM))).astype(BF16)
            k_s[a] = mixed[:, 128:256].astype(BF16)
            v_s[a, :, 0:128] = mixed[:, 256:384].astype(BF16)
            gate = jax.nn.sigmoid(mixed[:, 384:512])
            for r in range(ROWS):
                begin = pl.multiple_of(slot_of(r) * BAND, BAND)
                part = query[r * BAND : (r + 1) * BAND]
                for h in range(HEADS):
                    q_s[a, h, pl.ds(begin, BAND)] = jnp.where(own_lanes[h], part, jnp.zeros_like(part))
                g_s[pl.ds(pl.multiple_of(a * RES + begin, BAND), BAND)] = gate[r * BAND : (r + 1) * BAND]

    x_local.wait()
    project(0)

    def take(slot):
        shares[slot].wait_recv()
        begin = slot * BAND

        @pl.loop(0, HEADS)
        def _(h):
            for j in range(RES // 128):
                block = bands[slot, h, j * 128 : (j + 1) * 128].astype(F32)
                bias[h, begin : begin + BAND, j * 128 : (j + 1) * 128] = block.T

    arrive(1, 4, 5)
    arrive(2)
    arrive(3, 6)
    for slot in range(4):
        take(slot)

    def scores(step, h, j):
        phase, a = step // MINE, step % MINE
        rows = pl.ds(pl.multiple_of(phase * HALF, HALF), HALF)
        keys = slice(j * KC, (j + 1) * KC)
        logits = lax.dot_general(
            q_s[a, h, rows], k_s[a, keys], (((1,), (1,)), ((), ())), preferred_element_type=F32
        ) + bias[h, rows, keys]
        s_s[h % 2, :, keys] = logits
        most = logits[:, 0:128]
        for begin in range(128, KC, 128):
            most = jnp.maximum(most, logits[:, begin : begin + 128])
        m_s[h % 2] = most if j == 0 else jnp.maximum(m_s[h % 2], most)

    def soften(h, j):
        rows = slice(j * RC, (j + 1) * RC)
        most = jnp.max(m_s[h % 2, rows], axis=-1, keepdims=True)
        p_s[h % 2, rows] = jnp.exp(s_s[h % 2, rows] - most).astype(BF16)

    def attend(step, h):
        return jnp.dot(p_s[h % 2], v_s[step % MINE], preferred_element_type=F32)

    def settle(total, h):
        head = total[:, 0:128] / total[:, 128:256]
        acc_s[...] = head if h == 0 else jnp.where(own_lanes[h], head, acc_s[...])

    def produce(step):
        phase, a = step // MINE, step % MINE
        begin = pl.multiple_of(phase * HALF, HALF)
        gate = g_s[pl.ds(pl.multiple_of(a * RES + begin, HALF), HALF)]
        gated = (gate * acc_s[...]).astype(BF16)
        out_s[a, pl.ds(begin, HALF)] = jnp.dot(gated, wo_ref[...], preferred_element_type=F32).astype(BF16)

    band_rows = [row, row_z, row_1, row_3, (1 - zh) * 4 + row_1 % 4, (1 - zh) * 4 + row_3 % 4,
                 zh * 4 + (y + 2) % 4, (1 - zh) * 4 + (y + 2) % 4]

    def deliver(step):
        phase, a = step // MINE, step % MINE
        for slot in range(4):
            owner = jnp.where(phase == 0, band_rows[slot], band_rows[slot + 4])
            for half in range(2):
                to = owner * 2 + half
                begin = pl.multiple_of((phase * 4 + slot) * BAND + half * KEYS, KEYS)
                src, dst = out_s.at[a, pl.ds(begin, KEYS)], o_ref.at[col * MINE + a]

                @pl.when(to != col)
                def _():
                    remote(src, dst, o_send.at[to], o_recv.at[col], row, to).start()

                @pl.when(to == col)
                def _():
                    pltpu.make_async_copy(src, dst, o_own).start()

    for j in range(PARTS):
        scores(0, 0, j)

    steps = 2 * MINE

    @pl.loop(0, MINE)
    def _(turn):
        for part in (1, 2, 3):

            @pl.when(turn == part)
            def _():
                project(part)

        @pl.when(turn == 1)
        def _():
            arrive(4, 7)

        @pl.when(turn == 2)
        def _():
            arrive(5)
            arrive(6)

        @pl.when(turn == 3)
        def _():
            arrive(7)
            for slot in range(4, 8):
                take(slot)

        for index in range(2 * HEADS):
            h = index % HEADS
            step = turn * 2 + index // HEADS
            before, after = (step + steps - 1) % steps, (step + 1) % steps
            for j in range(PARTS):
                if h < HEADS - 1:
                    scores(step, h + 1, j)
                else:
                    scores(after, 0, j)
                soften(h, j)
                if j == 0:
                    total = attend(step if h else before, (h - 1) % HEADS)
            settle(total, (h - 1) % HEADS)
            if h == 0:
                produce(before)

        @pl.when(turn > 0)
        def _():
            deliver(turn * 2 - 1)

        deliver(turn * 2)

    last = steps - 1
    settle(attend(last, HEADS - 1), HEADS - 1)
    produce(last)
    deliver(last)

    for copy in sum(x_copies, []) + b_copies + list(relays.values()) + shares:
        copy.wait_send()
    for d in range(1, COLS):
        other = (col + d) % COLS
        block = o_ref.at[pl.ds(other * MINE, MINE)]
        remote(block, block, o_send.at[other], o_recv.at[other], row, other).wait()
    block = o_ref.at[pl.ds(col * MINE, MINE)]
    pltpu.make_async_copy(block, block, o_own).wait()


def shards(pair, ln_gain, w_query, w_key, w_value, w_gate, w_bias, w_out):
    dma = pltpu.SemaphoreType.DMA
    vmem = pl.BlockSpec(memory_space=pltpu.VMEM)
    return pl.pallas_call(
        kernel,
        out_shape=jax.ShapeDtypeStruct(pair.shape, BF16),
        in_specs=[vmem] * 8,
        out_specs=pl.BlockSpec(memory_space=pl.ANY),
        scratch_shapes=[
            pltpu.VMEM((MINE, RES, D), BF16),
            pltpu.VMEM((HEADS, KEYS, BAND), F32),
            pltpu.VMEM((HEADS, KEYS, BAND), BF16),
            pltpu.VMEM((SLOTS, HEADS, RES, BAND), BF16),
            pltpu.VMEM((HEADS, RES, RES), F32),
            pltpu.VMEM((D, 4 * D), BF16),
            pltpu.VMEM((MINE, HEADS, RES, D), BF16),
            pltpu.VMEM((MINE, RES, D), BF16),
            pltpu.VMEM((MINE, RES, 2 * D), BF16),
            pltpu.VMEM((MINE * RES, D), F32),
            pltpu.VMEM((2, HALF, RES), F32),
            pltpu.VMEM((2, HALF, RES), BF16),
            pltpu.VMEM((2, HALF, 128), F32),
            pltpu.VMEM((HALF, D), F32),
            pltpu.VMEM((MINE, RES, D), BF16),
            dma((4, COLS)), dma((4, COLS)), dma,
            dma((COLS,)), dma((COLS,)), dma,
            dma((7,)), dma((SLOTS,)),
            dma((SLOTS,)), dma((SLOTS,)),
            dma((COLS,)), dma((COLS,)), dma,
        ],
        compiler_params=pltpu.CompilerParams(
            collective_id=0, has_side_effects=True, vmem_limit_bytes=62 << 20
        ),
    )(
        pair, ln_gain.reshape(1, -1), w_query, w_key, w_value, w_gate, w_bias, w_out,
    )


def solution(mesh):
    return jax.shard_map(
        shards,
        mesh=mesh,
        in_specs=(P("row", "col", None), P(), P(), P(), P(), P(), P(), P()),
        out_specs=P("row", "col", None),
        check_vma=False,
    )
```

```python
import math

import jax
import jax.numpy as jnp
from jax import lax
from jax.experimental import pallas as pl
from jax.experimental.pallas import tpu as pltpu
from jax.sharding import PartitionSpec as P

F32 = jnp.float32
BF16 = jnp.bfloat16
MESH = pl.DeviceIdType.MESH

HEADS = 4
HEAD_DIM = 32
D = 128
RES = 1024
ROWS, COLS = 8, 16
BAND = RES // ROWS
KEYS = RES // COLS
MINE = BAND // COLS
SLOTS = 8
HALF = RES // 2
PARTS = 4
KC = RES // PARTS
RC = HALF // PARTS
SENT = [(0, 3), (3, 2), (5, 3)]
PROJECTED = [(0, 3), (3, 2), (5, 2), (7, 1)]
ORDER = [
    (1, 2, 0), (0, 1, 0), (1, 0, 0), (0, 3, 0), (1, 1, 0), (0, 2, 0), (1, 3, 0),
    (1, 2, 1), (0, 1, 1), (1, 0, 1), (0, 3, 1), (1, 1, 1), (0, 2, 1), (1, 3, 1), (0, 0, 1),
]


def layer_norm(tile, gain):
    values = tile.astype(F32)
    center = jnp.mean(values, axis=-1, keepdims=True)
    offset = values - center
    spread = jnp.mean(offset * offset, axis=-1, keepdims=True)
    return offset * lax.rsqrt(spread + 1e-05) * gain


def remote(src, dst, send, recv, row, col):
    return pltpu.make_async_remote_copy(
        src_ref=src, dst_ref=dst, send_sem=send, recv_sem=recv,
        device_id={"row": row, "col": col}, device_id_type=MESH,
    )


def kernel(
    x_ref, gain_ref, wq_ref, wk_ref, wv_ref, wg_ref, wb_ref, wo_ref, o_ref,
    got, piece_f, piece, bands, bias, w_all, q_s, k_s, v_s, g_s, s_s, p_s, m_s, acc_s, out_s,
    x_send, x_recv, x_own, b_send, b_recv, b_own, r_send, r_recv, c_send, c_recv, o_send, o_recv, o_own,
):
    row, col = lax.axis_index("row"), lax.axis_index("col")
    zh, y, core = row // 4, row % 4, col % 2
    row_z = (1 - zh) * 4 + y
    row_1 = zh * 4 + y + 1 - 2 * (y % 2)
    row_3 = zh * 4 + 3 - y
    col_c = col + 1 - 2 * core
    col_z = (col + 8) % COLS

    barrier = pltpu.get_barrier_semaphore()
    for d in range(1, COLS):
        pl.semaphore_signal(barrier, inc=1, device_id={"row": row, "col": (col + d) % COLS}, device_id_type=MESH)
    for other, at in ((row_z, col_z), (row_1, col), (row_3, col)):
        pl.semaphore_signal(barrier, inc=1, device_id={"row": other, "col": at}, device_id_type=MESH)

    own_keys = pl.ds(pl.multiple_of(col * KEYS, KEYS), KEYS)
    z_low, x_at = col // 8, (col // 2) % 4
    others = [
        ((z_low + dz) % 2) * 8 + ((x_at + dx) % 4) * 2 + (core + dc) % 2 for dz, dx, dc in ORDER
    ]

    def exchange(part):
        first, count = SENT[part]
        return [
            remote(
                x_ref.at[pl.ds(to * MINE + first, count)], got.at[pl.ds(first, count), own_keys],
                x_send.at[part, index], x_recv.at[part, index], row, to,
            )
            for index, to in enumerate(others)
        ]

    x_copies = [exchange(part) for part in range(3)]
    gain = gain_ref[...]
    acc_s[0:D] = jnp.zeros((D, D), F32)
    acc_s[0:D, 0:HEADS] = wb_ref[...].astype(F32)
    w_bias = acc_s[0:D].T[0:8].astype(BF16)

    pl.semaphore_wait(barrier, COLS - 1 + 3)
    for copy in x_copies[0]:
        copy.start()
    x_local = pltpu.make_async_copy(x_ref.at[pl.ds(col * MINE, MINE)], got.at[:, own_keys], x_own)
    x_local.start()

    @pl.loop(0, 8)
    def _(i):
        tile = x_ref[pl.ds(i * 16, 16)].reshape(16 * KEYS, D)
        g_s[pl.ds(pl.multiple_of(i * 16 * KEYS, 16 * KEYS), 16 * KEYS)] = layer_norm(tile, gain)

    @pl.loop(0, KEYS, unroll=8)
    def _(k):
        normed = g_s[pl.ds(k, BAND, stride=KEYS), :].astype(BF16)
        out = lax.dot_general(w_bias, normed, (((1,), (1,)), ((), ())), preferred_element_type=F32)
        for h in range(HEADS):
            piece_f[h, pl.ds(k, 1)] = out[h : h + 1]

    piece[...] = piece_f[...].astype(BF16)

    b_copies = []
    for index, to in enumerate(others):
        heads = pl.ds((to % 2) * 2, 2)
        copy = remote(piece.at[heads], bands.at[0, heads, own_keys], b_send.at[index], b_recv.at[index], row, to)
        copy.start()
        b_copies.append(copy)
    mine = pl.ds(core * 2, 2)
    b_local = pltpu.make_async_copy(piece.at[mine], bands.at[0, mine, own_keys], b_own)
    b_local.start()

    w_all[:, 0:128] = wq_ref[...]
    w_all[:, 128:256] = wk_ref[...]
    w_all[:, 256:384] = wv_ref[...]
    w_all[:, 384:512] = wg_ref[...]
    v_s[:, :, 128:] = jnp.ones((MINE, RES, 128), BF16)
    p_s[1] = jnp.ones((HALF, RES), BF16)

    b_local.wait()
    for copy in b_copies:
        copy.wait_recv()

    def band(slot):
        return bands.at[slot, mine]

    def relay(src, dst, index, to_row, to_col=col, heads=mine):
        return remote(
            bands.at[src, heads], bands.at[dst, heads], r_send.at[index], r_recv.at[index], to_row, to_col
        )

    def share(slot):
        return remote(band(slot), band(slot), c_send.at[slot], c_recv.at[slot], row, col_c)

    relays = {
        1: [relay(0, 1, 1, row_z, col_z)], 2: [relay(0, 2, 2, row_1)], 3: [relay(0, 3, 3, row_3)],
        4: [relay(1, 4, 4, row_1)], 5: [relay(3, 5, 5, row_z, col_z)], 6: [relay(2, 6, 6, row_3)],
        7: [
            relay(5, 7, 7, row_1, heads=pl.ds(core * 2, 1)),
            relay(4, 7, 0, row_3, heads=pl.ds(core * 2 + 1, 1)),
        ],
    }
    shares = [share(slot) for slot in range(SLOTS)]

    def arrive(slot, onward=None):
        for copy in relays[slot]:
            copy.wait_recv()
        if onward is not None:
            onward.start()
        shares[slot].start()

    for slot in (1, 2, 3):
        relays[slot][0].start()
    shares[0].start()
    for copy in x_copies[1] + x_copies[2]:
        copy.start()

    lane = lax.broadcasted_iota(jnp.int32, (1, D), 1)
    own_lanes = [(lane >= HEAD_DIM * h) & (lane < HEAD_DIM * (h + 1)) for h in range(HEADS)]

    def slot_of(band_row):
        z, w = band_row // 4, band_row % 4
        far, odd, high = (z + zh) % 2, (w + y) % 2, (w // 2 + y // 2) % 2
        near = odd * (2 + high + 2 * far)
        return near + (1 - odd) * (far + 6 * high)

    def project(part):
        if part < 3:
            for copy in x_copies[part]:
                copy.wait_recv()
        first, count = PROJECTED[part]

        @pl.loop(first, first + count)
        def _(a):
            normed = layer_norm(got[a], gain).astype(BF16)
            mixed = jnp.dot(normed, w_all[...], preferred_element_type=F32)
            query = (mixed[:, 0:128] * (1.0 / math.sqrt(HEAD_DIM))).astype(BF16)
            k_s[a] = mixed[:, 128:256].astype(BF16)
            v_s[a, :, 0:128] = mixed[:, 256:384].astype(BF16)
            gate = jax.nn.sigmoid(mixed[:, 384:512])
            for r in range(ROWS):
                begin = pl.multiple_of(slot_of(r) * BAND, BAND)
                part = query[r * BAND : (r + 1) * BAND]
                for h in range(HEADS):
                    q_s[a, h, pl.ds(begin, BAND)] = jnp.where(own_lanes[h], part, jnp.zeros_like(part))
                g_s[pl.ds(pl.multiple_of(a * RES + begin, BAND), BAND)] = gate[r * BAND : (r + 1) * BAND]

    x_local.wait()
    project(0)

    def take(slot):
        shares[slot].wait_recv()
        begin = slot * BAND

        @pl.loop(0, HEADS)
        def _(h):
            for j in range(RES // 128):
                block = bands[slot, h, j * 128 : (j + 1) * 128].astype(F32)
                bias[h, begin : begin + BAND, j * 128 : (j + 1) * 128] = block.T

    arrive(1, relays[4][0])
    arrive(2, relays[6][0])
    arrive(3, relays[5][0])
    for slot in range(4):
        take(slot)

    def scores(step, h, j):
        phase, a = step // MINE, step % MINE
        rows = pl.ds(pl.multiple_of(phase * HALF, HALF), HALF)
        keys = slice(j * KC, (j + 1) * KC)
        logits = lax.dot_general(
            q_s[a, h, rows], k_s[a, keys], (((1,), (1,)), ((), ())), preferred_element_type=F32
        ) + bias[h, rows, keys]
        s_s[h % 2, :, keys] = logits
        most = logits[:, 0:128]
        for begin in range(128, KC, 128):
            most = jnp.maximum(most, logits[:, begin : begin + 128])
        m_s[h % 2] = most if j == 0 else jnp.maximum(m_s[h % 2], most)

    def soften(h, j):
        rows = slice(j * RC, (j + 1) * RC)
        most = jnp.max(m_s[h % 2, rows], axis=-1, keepdims=True)
        p_s[h % 2, rows] = jnp.exp(s_s[h % 2, rows] - most).astype(BF16)

    def attend(step, h):
        return jnp.dot(p_s[h % 2], v_s[step % MINE], preferred_element_type=F32)

    def settle(total, h):
        head = total[:, 0:128] / total[:, 128:256]
        acc_s[...] = head if h == 0 else jnp.where(own_lanes[h], head, acc_s[...])

    def produce(step):
        phase, a = step // MINE, step % MINE
        begin = pl.multiple_of(phase * HALF, HALF)
        gate = g_s[pl.ds(pl.multiple_of(a * RES + begin, HALF), HALF)]
        gated = (gate * acc_s[...]).astype(BF16)
        out_s[a, pl.ds(begin, HALF)] = jnp.dot(gated, wo_ref[...], preferred_element_type=F32).astype(BF16)

    band_rows = [row, row_z, row_1, row_3, (1 - zh) * 4 + row_1 % 4, (1 - zh) * 4 + row_3 % 4,
                 zh * 4 + (y + 2) % 4, (1 - zh) * 4 + (y + 2) % 4]

    def deliver(step):
        phase, a = step // MINE, step % MINE
        for slot in range(4):
            owner = jnp.where(phase == 0, band_rows[slot], band_rows[slot + 4])
            for half in range(2):
                to = owner * 2 + half
                begin = pl.multiple_of((phase * 4 + slot) * BAND + half * KEYS, KEYS)
                src, dst = out_s.at[a, pl.ds(begin, KEYS)], o_ref.at[col * MINE + a]

                @pl.when(to != col)
                def _():
                    remote(src, dst, o_send.at[to], o_recv.at[col], row, to).start()

                @pl.when(to == col)
                def _():
                    pltpu.make_async_copy(src, dst, o_own).start()

    for j in range(PARTS):
        scores(0, 0, j)

    steps = 2 * MINE

    @pl.loop(0, MINE)
    def _(turn):
        for part in (1, 2, 3):

            @pl.when(turn == part)
            def _():
                project(part)

        @pl.when(turn == 1)
        def _():
            arrive(4, relays[7][1])
            arrive(5, relays[7][0])

        @pl.when(turn == 2)
        def _():
            arrive(6)

        @pl.when(turn == 3)
        def _():
            arrive(7)
            for slot in range(4, 8):
                take(slot)

        for index in range(2 * HEADS):
            h = index % HEADS
            step = turn * 2 + index // HEADS
            before, after = (step + steps - 1) % steps, (step + 1) % steps
            for j in range(PARTS):
                if h < HEADS - 1:
                    scores(step, h + 1, j)
                else:
                    scores(after, 0, j)
                soften(h, j)
                if j == 0:
                    total = attend(step if h else before, (h - 1) % HEADS)
            settle(total, (h - 1) % HEADS)
            if h == 0:
                produce(before)

        @pl.when(turn > 0)
        def _():
            deliver(turn * 2 - 1)

        deliver(turn * 2)

    last = steps - 1
    settle(attend(last, HEADS - 1), HEADS - 1)
    produce(last)
    deliver(last)

    for copy in sum(x_copies, []) + b_copies + sum(relays.values(), []) + shares:
        copy.wait_send()
    for d in range(1, COLS):
        other = (col + d) % COLS
        block = o_ref.at[pl.ds(other * MINE, MINE)]
        remote(block, block, o_send.at[other], o_recv.at[other], row, other).wait()
    block = o_ref.at[pl.ds(col * MINE, MINE)]
    pltpu.make_async_copy(block, block, o_own).wait()


def shards(pair, ln_gain, w_query, w_key, w_value, w_gate, w_bias, w_out):
    dma = pltpu.SemaphoreType.DMA
    vmem = pl.BlockSpec(memory_space=pltpu.VMEM)
    return pl.pallas_call(
        kernel,
        out_shape=jax.ShapeDtypeStruct(pair.shape, BF16),
        in_specs=[vmem] * 8,
        out_specs=pl.BlockSpec(memory_space=pl.ANY),
        scratch_shapes=[
            pltpu.VMEM((MINE, RES, D), BF16),
            pltpu.VMEM((HEADS, KEYS, BAND), F32),
            pltpu.VMEM((HEADS, KEYS, BAND), BF16),
            pltpu.VMEM((SLOTS, HEADS, RES, BAND), BF16),
            pltpu.VMEM((HEADS, RES, RES), F32),
            pltpu.VMEM((D, 4 * D), BF16),
            pltpu.VMEM((MINE, HEADS, RES, D), BF16),
            pltpu.VMEM((MINE, RES, D), BF16),
            pltpu.VMEM((MINE, RES, 2 * D), BF16),
            pltpu.VMEM((MINE * RES, D), F32),
            pltpu.VMEM((2, HALF, RES), F32),
            pltpu.VMEM((2, HALF, RES), BF16),
            pltpu.VMEM((2, HALF, 128), F32),
            pltpu.VMEM((HALF, D), F32),
            pltpu.VMEM((MINE, RES, D), BF16),
            dma((3, COLS)), dma((3, COLS)), dma,
            dma((COLS,)), dma((COLS,)), dma,
            dma((SLOTS,)), dma((SLOTS,)),
            dma((SLOTS,)), dma((SLOTS,)),
            dma((COLS,)), dma((COLS,)), dma,
        ],
        compiler_params=pltpu.CompilerParams(
            collective_id=0, has_side_effects=True, vmem_limit_bytes=62 << 20
        ),
    )(
        pair, ln_gain.reshape(1, -1), w_query, w_key, w_value, w_gate, w_bias, w_out,
    )


def solution(mesh):
    return jax.shard_map(
        shards,
        mesh=mesh,
        in_specs=(P("row", "col", None), P(), P(), P(), P(), P(), P(), P()),
        out_specs=P("row", "col", None),
        check_vma=False,
    )
```

```python
import math

import jax
import jax.numpy as jnp
from jax import lax
from jax.experimental import pallas as pl
from jax.experimental.pallas import tpu as pltpu
from jax.sharding import PartitionSpec as P

F32 = jnp.float32
BF16 = jnp.bfloat16
MESH = pl.DeviceIdType.MESH

HEADS = 4
HEAD_DIM = 32
D = 128
RES = 1024
ROWS, COLS = 8, 16
BAND = RES // ROWS
KEYS = RES // COLS
MINE = BAND // COLS
SLOTS = 8
HALF = RES // 2
PARTS = 4
KC = RES // PARTS
RC = HALF // PARTS
SENT = [(0, 3), (3, 2), (5, 3)]
PROJECTED = [(0, 3), (3, 2), (5, 2), (7, 1)]
ORDER = [
    (1, 2, 0), (0, 1, 0), (1, 0, 0), (0, 3, 0), (1, 1, 0), (0, 2, 0), (1, 3, 0),
    (1, 2, 1), (0, 1, 1), (1, 0, 1), (0, 3, 1), (1, 1, 1), (0, 2, 1), (1, 3, 1), (0, 0, 1),
]


def layer_norm(tile, gain):
    values = tile.astype(F32)
    center = jnp.mean(values, axis=-1, keepdims=True)
    offset = values - center
    spread = jnp.mean(offset * offset, axis=-1, keepdims=True)
    return offset * lax.rsqrt(spread + 1e-05) * gain


def remote(src, dst, send, recv, row, col):
    return pltpu.make_async_remote_copy(
        src_ref=src, dst_ref=dst, send_sem=send, recv_sem=recv,
        device_id={"row": row, "col": col}, device_id_type=MESH,
    )


def kernel(
    x_ref, gain_ref, wq_ref, wk_ref, wv_ref, wg_ref, wb_ref, wo_ref, o_ref,
    got, piece_f, piece, bands, bias, w_all, q_s, k_s, v_s, g_s, s_s, p_s, m_s, acc_s, out_s,
    x_send, x_recv, x_own, b_send, b_recv, b_own, r_send, r_recv, c_send, c_recv, o_send, o_recv, o_own,
):
    row, col = lax.axis_index("row"), lax.axis_index("col")
    zh, y, core = row // 4, row % 4, col % 2
    row_z = (1 - zh) * 4 + y
    row_1 = zh * 4 + y + 1 - 2 * (y % 2)
    row_3 = zh * 4 + 3 - y
    col_c = col + 1 - 2 * core
    col_z = (col + 8) % COLS

    barrier = pltpu.get_barrier_semaphore()
    for d in range(1, COLS):
        pl.semaphore_signal(barrier, inc=1, device_id={"row": row, "col": (col + d) % COLS}, device_id_type=MESH)
    for other, at in ((row_z, col_z), (row_1, col), (row_3, col)):
        pl.semaphore_signal(barrier, inc=1, device_id={"row": other, "col": at}, device_id_type=MESH)

    own_keys = pl.ds(pl.multiple_of(col * KEYS, KEYS), KEYS)
    z_low, x_at = col // 8, (col // 2) % 4
    others = [
        ((z_low + dz) % 2) * 8 + ((x_at + dx) % 4) * 2 + (core + dc) % 2 for dz, dx, dc in ORDER
    ]

    def exchange(part):
        first, count = SENT[part]
        return [
            remote(
                x_ref.at[pl.ds(to * MINE + first, count)], got.at[pl.ds(first, count), own_keys],
                x_send.at[part, index], x_recv.at[part, index], row, to,
            )
            for index, to in enumerate(others)
        ]

    x_copies = [exchange(part) for part in range(3)]
    gain = gain_ref[...]
    acc_s[0:D] = jnp.zeros((D, D), F32)
    acc_s[0:D, 0:HEADS] = wb_ref[...].astype(F32)
    w_bias = acc_s[0:D].T[0:8].astype(BF16)

    pl.semaphore_wait(barrier, COLS - 1 + 3)
    for copy in x_copies[0]:
        copy.start()
    x_local = pltpu.make_async_copy(x_ref.at[pl.ds(col * MINE, MINE)], got.at[:, own_keys], x_own)
    x_local.start()

    @pl.loop(0, 8, unroll=2)
    def _(i):
        tile = x_ref[pl.ds(i * 16, 16)].reshape(16 * KEYS, D)
        g_s[pl.ds(pl.multiple_of(i * 16 * KEYS, 16 * KEYS), 16 * KEYS)] = layer_norm(tile, gain)

    @pl.loop(0, KEYS, unroll=16)
    def _(k):
        normed = g_s[pl.ds(k, BAND, stride=KEYS), :].astype(BF16)
        out = lax.dot_general(w_bias, normed, (((1,), (1,)), ((), ())), preferred_element_type=F32)
        for h in range(HEADS):
            piece_f[h, pl.ds(k, 1)] = out[h : h + 1]

    piece[...] = piece_f[...].astype(BF16)

    b_copies = [
        [
            remote(
                piece.at[pl.ds((to % 2) * 2 + part, 1)], bands.at[0, pl.ds((to % 2) * 2 + part, 1), own_keys],
                b_send.at[part, index], b_recv.at[part, index], row, to,
            )
            for index, to in enumerate(others)
        ]
        for part in range(2)
    ]
    for copy in b_copies[0] + b_copies[1]:
        copy.start()
    mine = pl.ds(core * 2, 2)
    b_local = pltpu.make_async_copy(piece.at[mine], bands.at[0, mine, own_keys], b_own)
    b_local.start()

    w_all[:, 0:128] = wq_ref[...]
    w_all[:, 128:256] = wk_ref[...]
    w_all[:, 256:384] = wv_ref[...]
    w_all[:, 384:512] = wg_ref[...]
    v_s[:, :, 128:] = jnp.ones((MINE, RES, 128), BF16)
    p_s[1] = jnp.ones((HALF, RES), BF16)

    def relay(src, dst, index, to_row, to_col=col, heads=mine):
        return remote(
            bands.at[src, heads], bands.at[dst, heads], r_send.at[index], r_recv.at[index], to_row, to_col
        )

    def share(slot):
        band = bands.at[slot, mine]
        return remote(band, band, c_send.at[slot], c_recv.at[slot], row, col_c)

    single = [pl.ds(core * 2 + part, 1) for part in range(2)]
    relays = {
        1: [relay(0, 1, part, row_z, col_z, single[part]) for part in range(2)],
        2: [relay(0, 2, 2 + part, row_1, col, single[part]) for part in range(2)],
        3: [relay(0, 3, 8 + part, row_3, col, single[part]) for part in range(2)],
        4: [relay(1, 4, 4, row_1)], 5: [relay(3, 5, 5, row_z, col_z)], 6: [relay(2, 6, 6, row_3)],
        7: [
            relay(5, 7, 7, row_1, heads=single[0]),
            relay(4, 7, 10, row_3, heads=single[1]),
        ],
    }
    shares = [share(slot) for slot in range(SLOTS)]

    def arrive(slot, onward=None):
        for copy in relays[slot]:
            copy.wait_recv()
        if onward is not None:
            onward.start()
        shares[slot].start()

    b_local.wait()
    for part in range(2):
        for copy in b_copies[part]:
            copy.wait_recv()
        for slot in (1, 2, 3):
            relays[slot][part].start()
    shares[0].start()
    for copy in x_copies[1] + x_copies[2]:
        copy.start()

    lane = lax.broadcasted_iota(jnp.int32, (1, D), 1)
    own_lanes = [(lane >= HEAD_DIM * h) & (lane < HEAD_DIM * (h + 1)) for h in range(HEADS)]

    def slot_of(band_row):
        z, w = band_row // 4, band_row % 4
        far, odd, high = (z + zh) % 2, (w + y) % 2, (w // 2 + y // 2) % 2
        near = odd * (2 + high + 2 * far)
        return near + (1 - odd) * (far + 6 * high)

    def project(part):
        if part < 3:
            for copy in x_copies[part]:
                copy.wait_recv()
        first, count = PROJECTED[part]

        @pl.loop(first, first + count)
        def _(a):
            normed = layer_norm(got[a], gain).astype(BF16)
            mixed = jnp.dot(normed, w_all[...], preferred_element_type=F32)
            query = (mixed[:, 0:128] * (1.0 / math.sqrt(HEAD_DIM))).astype(BF16)
            k_s[a] = mixed[:, 128:256].astype(BF16)
            v_s[a, :, 0:128] = mixed[:, 256:384].astype(BF16)
            gate = jax.nn.sigmoid(mixed[:, 384:512])
            for r in range(ROWS):
                begin = pl.multiple_of(slot_of(r) * BAND, BAND)
                part = query[r * BAND : (r + 1) * BAND]
                for h in range(HEADS):
                    q_s[a, h, pl.ds(begin, BAND)] = jnp.where(own_lanes[h], part, jnp.zeros_like(part))
                g_s[pl.ds(pl.multiple_of(a * RES + begin, BAND), BAND)] = gate[r * BAND : (r + 1) * BAND]

    x_local.wait()
    def take(slot):
        shares[slot].wait_recv()
        begin = slot * BAND

        @pl.loop(0, HEADS)
        def _(h):
            for j in range(RES // 128):
                block = bands[slot, h, j * 128 : (j + 1) * 128].astype(F32)
                bias[h, begin : begin + BAND, j * 128 : (j + 1) * 128] = block.T

    project(0)
    take(0)

    arrive(1, relays[4][0])
    arrive(2, relays[6][0])
    arrive(3, relays[5][0])
    for slot in (1, 2, 3):
        take(slot)

    def scores(step, h, j):
        phase, a = step // MINE, step % MINE
        rows = pl.ds(pl.multiple_of(phase * HALF, HALF), HALF)
        keys = slice(j * KC, (j + 1) * KC)
        logits = lax.dot_general(
            q_s[a, h, rows], k_s[a, keys], (((1,), (1,)), ((), ())), preferred_element_type=F32
        ) + bias[h, rows, keys]
        s_s[h % 2, :, keys] = logits
        most = logits[:, 0:128]
        for begin in range(128, KC, 128):
            most = jnp.maximum(most, logits[:, begin : begin + 128])
        m_s[h % 2] = most if j == 0 else jnp.maximum(m_s[h % 2], most)

    def soften(h, j):
        rows = slice(j * RC, (j + 1) * RC)
        most = jnp.max(m_s[h % 2, rows], axis=-1, keepdims=True)
        p_s[h % 2, rows] = jnp.exp(s_s[h % 2, rows] - most).astype(BF16)

    def attend(step, h):
        return jnp.dot(p_s[h % 2], v_s[step % MINE], preferred_element_type=F32)

    def settle(total, h):
        head = total[:, 0:128] / total[:, 128:256]
        acc_s[...] = head if h == 0 else jnp.where(own_lanes[h], head, acc_s[...])

    def produce(step):
        phase, a = step // MINE, step % MINE
        begin = pl.multiple_of(phase * HALF, HALF)
        gate = g_s[pl.ds(pl.multiple_of(a * RES + begin, HALF), HALF)]
        gated = (gate * acc_s[...]).astype(BF16)
        out_s[a, pl.ds(begin, HALF)] = jnp.dot(gated, wo_ref[...], preferred_element_type=F32).astype(BF16)

    band_rows = [row, row_z, row_1, row_3, (1 - zh) * 4 + row_1 % 4, (1 - zh) * 4 + row_3 % 4,
                 zh * 4 + (y + 2) % 4, (1 - zh) * 4 + (y + 2) % 4]

    def deliver(step):
        phase, a = step // MINE, step % MINE
        for slot in range(4):
            owner = jnp.where(phase == 0, band_rows[slot], band_rows[slot + 4])
            for half in range(2):
                to = owner * 2 + half
                begin = pl.multiple_of((phase * 4 + slot) * BAND + half * KEYS, KEYS)
                src, dst = out_s.at[a, pl.ds(begin, KEYS)], o_ref.at[col * MINE + a]

                @pl.when(to != col)
                def _():
                    remote(src, dst, o_send.at[to], o_recv.at[col], row, to).start()

                @pl.when(to == col)
                def _():
                    pltpu.make_async_copy(src, dst, o_own).start()

    for j in range(PARTS):
        scores(0, 0, j)

    steps = 2 * MINE

    @pl.loop(0, MINE)
    def _(turn):
        for part in (1, 2, 3):

            @pl.when(turn == part)
            def _():
                project(part)

        @pl.when(turn == 2)
        def _():
            arrive(4, relays[7][1])
            arrive(5, relays[7][0])
            arrive(6)

        @pl.when(turn == 3)
        def _():
            arrive(7)
            for slot in range(4, 8):
                take(slot)

        for index in range(2 * HEADS):
            h = index % HEADS
            step = turn * 2 + index // HEADS
            before, after = (step + steps - 1) % steps, (step + 1) % steps
            for j in range(PARTS):
                if h < HEADS - 1:
                    scores(step, h + 1, j)
                else:
                    scores(after, 0, j)
                soften(h, j)
                if j == 0:
                    total = attend(step if h else before, (h - 1) % HEADS)
            settle(total, (h - 1) % HEADS)
            if h == 0:
                produce(before)

        @pl.when(turn > 0)
        def _():
            deliver(turn * 2 - 1)

        deliver(turn * 2)

    last = steps - 1
    settle(attend(last, HEADS - 1), HEADS - 1)
    produce(last)
    deliver(last)

    for copy in sum(x_copies, []) + sum(b_copies, []) + sum(relays.values(), []) + shares:
        copy.wait_send()
    for d in range(1, COLS):
        other = (col + d) % COLS
        block = o_ref.at[pl.ds(other * MINE, MINE)]
        remote(block, block, o_send.at[other], o_recv.at[other], row, other).wait()
    block = o_ref.at[pl.ds(col * MINE, MINE)]
    pltpu.make_async_copy(block, block, o_own).wait()


def shards(pair, ln_gain, w_query, w_key, w_value, w_gate, w_bias, w_out):
    dma = pltpu.SemaphoreType.DMA
    vmem = pl.BlockSpec(memory_space=pltpu.VMEM)
    return pl.pallas_call(
        kernel,
        out_shape=jax.ShapeDtypeStruct(pair.shape, BF16),
        in_specs=[vmem] * 8,
        out_specs=pl.BlockSpec(memory_space=pl.ANY),
        scratch_shapes=[
            pltpu.VMEM((MINE, RES, D), BF16),
            pltpu.VMEM((HEADS, KEYS, BAND), F32),
            pltpu.VMEM((HEADS, KEYS, BAND), BF16),
            pltpu.VMEM((SLOTS, HEADS, RES, BAND), BF16),
            pltpu.VMEM((HEADS, RES, RES), F32),
            pltpu.VMEM((D, 4 * D), BF16),
            pltpu.VMEM((MINE, HEADS, RES, D), BF16),
            pltpu.VMEM((MINE, RES, D), BF16),
            pltpu.VMEM((MINE, RES, 2 * D), BF16),
            pltpu.VMEM((MINE * RES, D), F32),
            pltpu.VMEM((2, HALF, RES), F32),
            pltpu.VMEM((2, HALF, RES), BF16),
            pltpu.VMEM((2, HALF, 128), F32),
            pltpu.VMEM((HALF, D), F32),
            pltpu.VMEM((MINE, RES, D), BF16),
            dma((3, COLS)), dma((3, COLS)), dma,
            dma((2, COLS)), dma((2, COLS)), dma,
            dma((11,)), dma((11,)),
            dma((SLOTS,)), dma((SLOTS,)),
            dma((COLS,)), dma((COLS,)), dma,
        ],
        compiler_params=pltpu.CompilerParams(
            collective_id=0, has_side_effects=True, vmem_limit_bytes=62 << 20
        ),
    )(
        pair, ln_gain.reshape(1, -1), w_query, w_key, w_value, w_gate, w_bias, w_out,
    )


def solution(mesh):
    return jax.shard_map(
        shards,
        mesh=mesh,
        in_specs=(P("row", "col", None), P(), P(), P(), P(), P(), P(), P()),
        out_specs=P("row", "col", None),
        check_vma=False,
    )
```
